32 devices in a mesh: parts: 2 (over y), replica: 4 (over z), tensor: 4 (over x, core).
Axes of the slice: x: 2, y: 2, z: 4, core: 2. Of those that a mesh axis runs over, the one named last changes fastest.
Arguments:
- attention_rows: bfloat16 [2048, 8192], P(('parts', 'replica'), 'tensor'), parts along dimension 0, may hold values from -6 to 6
- output_projection_weight: bfloat16 [8192, 8192], P('tensor', 'replica'), may hold values from -0.0625 to 0.0625
- adapter_down_factors: bfloat16 [256, 16, 8192], P('replica', None, 'tensor'), may hold values from -0.0625 to 0.0625
- adapter_up_factors: bfloat16 [256, 16, 8192], P('tensor', None, 'replica'), may hold values from -1.5 to 1.5
- row_segment_slot: int32 [2048], P('parts'), parts along dimension 0, may hold values from 0 to 15, as said below
- segment_slot_adapter: int32 [8, 16], P('parts'), parts along dimension 0, may hold values from -1 to 255, as said below
Outputs:
- projected: bfloat16 [2048, 8192], P(('parts', 'tensor'), 'replica'), parts along dimension 0
The draws below stay inside these ranges and needn't reach their ends.
There are 2 independent parts, one for each index of `parts`. The reference program is written for one: setup_inputs(seed, part) draws one part's arguments, and reference() takes and returns one part's arrays. A program takes and returns all parts, laid end to end along the dimension named above; an argument that names none is the same for every part. Nothing has to cross between parts.
Inputs may be any that keep to these rules, and one draw needn't show every extreme that they name: row_segment_slot[i] names a slot of row i // 256 of segment_slot_adapter that is not -1; when 256 is at least the number of such slots, every one of them is named by some row of that group. `segment_slot_adapter`: in each row g, slots o * 4 to o * 4 + 3 hold distinct adapters of o * 64 to (o + 1) * 64 - 1, filled slots first, then -1; in every draw some owner o has all 4 slots filled in every row, and every row has some owner with all 4 slots filled.
All inputs are finite; a program needn't handle non-finite values.
Results may differ from the reference program's by a relative error of at most 0.0065.
Values may be sent and summed in bfloat16 or wider, within the bound.
A program may use at most 128 MiB of HBM per device.

```python
import jax
import jax.numpy as jnp
from jax import lax

MODEL_WIDTH = 8192
QUERY_HEADS = 64
HEAD_WIDTH = 128
ADAPTER_RANK = 16
ROWS_DEV = 256
ADP_DEV = 64
CAP = 4
ROWS_ALL = 1024
ADAPTER_TOTAL = 256
N_REPLICA = 4
N_TENSOR = 4


def adapter_plan(key):
    key_list = jax.random.split(key, 6)
    owner_index = jnp.arange(N_REPLICA, dtype=jnp.int32)
    group_index = jnp.arange(N_REPLICA, dtype=jnp.int32)
    live_count = jax.random.randint(key_list[0], (N_REPLICA, N_REPLICA), 1, CAP + 1)
    full_owner = jax.random.randint(key_list[1], (), 0, N_REPLICA)
    group_full = jax.random.randint(key_list[2], (N_REPLICA,), 0, N_REPLICA)
    live_count = jnp.where(owner_index[None, :] == full_owner, CAP, live_count)
    live_count = jnp.where(owner_index[None, :] == group_full[:, None], CAP, live_count)
    first_group = group_index[:, None] == 0
    live_count = jnp.where(first_group & (owner_index[None, :] == N_REPLICA - 1), CAP, live_count)
    next_owner = (full_owner + 1) % N_REPLICA
    pad_owner = jnp.where(next_owner == N_REPLICA - 1, (full_owner + 2) % N_REPLICA, next_owner)
    live_count = jnp.where(first_group & (owner_index[None, :] == pad_owner), 1, live_count)
    scores = jax.random.randint(key_list[3], (N_REPLICA, N_REPLICA, ADP_DEV), 0, 1 << 20) * ADP_DEV
    local_index = jnp.arange(ADP_DEV, dtype=jnp.int32)
    scores = scores + local_index
    forced = (group_index[:, None, None] == 0) & (owner_index[None, :, None] == N_REPLICA - 1) & (local_index[None, None, :] == ADP_DEV - 1)
    scores = jnp.where(forced, -1, scores)
    local_pick = jnp.argsort(scores, axis=-1)[:, :, :CAP].astype(jnp.int32)
    adapter_ids = owner_index[None, :, None] * ADP_DEV + local_pick
    live_slot = jnp.arange(CAP, dtype=jnp.int32)[None, None, :] < live_count[:, :, None]
    slot_table = jnp.where(live_slot, adapter_ids, -1).reshape(N_REPLICA, N_REPLICA * CAP).astype(jnp.int32)
    live_flat = live_slot.reshape(N_REPLICA, N_REPLICA * CAP).astype(jnp.int32)
    live_rank = jnp.cumsum(live_flat, axis=1) - 1
    live_total = jnp.sum(live_flat, axis=1)
    row_index = jnp.arange(ROWS_DEV, dtype=jnp.int32)
    spare_rank = jax.random.randint(key_list[4], (N_REPLICA, ROWS_DEV), 0, 1 << 20) % live_total[:, None]
    rank_wanted = jnp.where(row_index[None, :] < live_total[:, None], row_index[None, :], spare_rank)
    slot_hits = (live_rank[:, None, :] == rank_wanted[:, :, None]) & (live_flat[:, None, :] == 1)
    slot_chosen = jnp.argmax(slot_hits.astype(jnp.int32), axis=-1).astype(jnp.int32)
    order_keys = jax.random.randint(key_list[5], (N_REPLICA, ROWS_DEV), 0, 1 << 20) * ROWS_DEV + row_index[None, :]
    row_order = jnp.argsort(order_keys, axis=-1)
    shuffled = jnp.take_along_axis(slot_chosen, row_order, axis=1)
    return (slot_table, shuffled.reshape(N_REPLICA * ROWS_DEV).astype(jnp.int32))


def draw_row_segment_slot(key, part):
    return adapter_plan(key)[1]


def draw_segment_slot_adapter(key, part):
    return adapter_plan(key)[0]


def shard_levels(rng, extent, shards, least, largest):
    def one(dim, parts):
        heights = jax.random.uniform(jax.random.fold_in(jax.random.fold_in(rng, 6), dim), (parts,), jnp.float32, least / len(shards), largest / len(shards))
        return jnp.repeat(jnp.exp(heights), extent[dim] // parts).reshape((-1,) + (1,) * (len(extent) - dim - 1))

    gain = one(*shards[0])
    for cut in shards[1:]:
        gain = gain * one(*cut)
    return gain


def centred(stream_key, dims, spread, most, cuts=(), kind=jnp.bfloat16):
    array = spread * jax.random.normal(stream_key, dims, jnp.float32)
    if cuts:
        array = array * shard_levels(stream_key, dims, cuts, -0.22, 0.18)
    return jnp.clip(array, -most, most).astype(kind)


def setup_inputs(seed: int = 0, part: int = 0) -> dict:
    keys = jax.random.split(jax.random.key(seed), 7)
    part_splits = jax.random.split(jax.random.fold_in(keys[6], part), 7)
    attention_rows = centred(part_splits[0], (ROWS_ALL, QUERY_HEADS * HEAD_WIDTH), 1.0, 6.0, ((0, 4), (1, 4)))
    output_projection_weight = centred(keys[1], (QUERY_HEADS * HEAD_WIDTH, MODEL_WIDTH), (QUERY_HEADS * HEAD_WIDTH) ** -0.5, 0.0625, ((0, 4), (1, 4)))
    adapter_down_factors = centred(keys[2], (ADAPTER_TOTAL, ADAPTER_RANK, QUERY_HEADS * HEAD_WIDTH), (QUERY_HEADS * HEAD_WIDTH) ** -0.5, 0.0625, ((0, 4), (2, 4)))
    adapter_up_factors = centred(keys[3], (ADAPTER_TOTAL, ADAPTER_RANK, MODEL_WIDTH), ADAPTER_RANK ** -0.5, 1.5, ((0, 4), (2, 4)))
    row_segment_slot = draw_row_segment_slot(jax.random.fold_in(jax.random.fold_in(keys[6], part), 71), part)
    segment_slot_adapter = draw_segment_slot_adapter(jax.random.fold_in(jax.random.fold_in(keys[6], part), 71), part)
    return dict(attention_rows=attention_rows, output_projection_weight=output_projection_weight, adapter_down_factors=adapter_down_factors, adapter_up_factors=adapter_up_factors, row_segment_slot=row_segment_slot, segment_slot_adapter=segment_slot_adapter)


adapter_scale = 2.0


def reference(attention_rows, output_projection_weight, adapter_down_factors, adapter_up_factors, row_segment_slot, segment_slot_adapter):
    row_total = attention_rows.shape[0]
    width = attention_rows.shape[1] // N_TENSOR
    group_of = (jnp.arange(row_total, dtype=jnp.int32) // ROWS_DEV).astype(jnp.int32)
    adapter = segment_slot_adapter[group_of, row_segment_slot].astype(jnp.int32)

    def add_share(total, index):
        begin = (index * width).astype(jnp.int32)
        columns = lax.dynamic_slice_in_dim(attention_rows, begin, width, 1)
        weights = lax.dynamic_slice_in_dim(output_projection_weight, begin, width, 0)
        share = jnp.dot(columns, weights, preferred_element_type=jnp.float32).astype(jnp.bfloat16)
        share = lax.optimization_barrier(share)
        return total + share.astype(jnp.float32), None

    zero_sum = jnp.zeros((row_total, output_projection_weight.shape[1]), jnp.float32)
    base_output, _ = lax.scan(add_share, zero_sum, jnp.arange(N_TENSOR, dtype=jnp.int32))

    def group_delta(index):
        begin = (index * ROWS_DEV).astype(jnp.int32)
        rows_here = lax.dynamic_slice_in_dim(attention_rows, begin, ROWS_DEV, 0).astype(jnp.float32)
        adapter_index_local = lax.dynamic_slice_in_dim(adapter, begin, ROWS_DEV, 0).astype(jnp.int32)
        down_factor_local = jnp.take(adapter_down_factors, adapter_index_local, axis=0).astype(jnp.float32)
        shrink = jnp.einsum("rkc,rc->rk", down_factor_local, rows_here).astype(jnp.bfloat16)
        up_factor_local = jnp.take(adapter_up_factors, adapter_index_local, axis=0).astype(jnp.float32)
        return jnp.einsum("rk,rkd->rd", shrink.astype(jnp.float32), up_factor_local)

    adapter_delta = lax.map(group_delta, jnp.arange(N_REPLICA, dtype=jnp.int32))
    adapter_delta = adapter_delta.reshape(row_total, output_projection_weight.shape[1])
    return (base_output + adapter_scale * adapter_delta).astype(jnp.bfloat16)
```

```python
import functools

import jax
import jax.numpy as jnp
from jax import lax
from jax.experimental import pallas as pl
from jax.experimental.pallas import tpu as pltpu
from jax.sharding import PartitionSpec as P

MESH = pl.DeviceIdType.MESH
adapter_scale = 2.0
row_chunk = 64
tile_width = 1024


def kernel(
    groups, peers, chunks, tiles,
    table, slots, x_hbm, w_hbm, down_hbm, up_hbm,
    out,
    x_all, w_all, down, up, down_sel, up_send, up_got,
    share_out, share_got, rank_out, rank_got, fin_out, fin_got, delta,
    load_sem, x_right_sem, x_left_sem, x_recv_sem,
    up_send_sem, up_recv_sem, share_send_sem, share_recv_sem,
    rank_send_sem, rank_recv_sem, fin_send_sem, fin_recv_sem,
):
    z = lax.axis_index("replica")
    t = lax.axis_index("tensor")
    owned, rank, width = down.shape
    cap = table.shape[1] // groups
    rows = x_all.shape[2]

    barrier = pltpu.get_barrier_semaphore()
    for d in range(1, groups):
        pl.semaphore_signal(
            barrier, inc=1, device_id={"replica": lax.rem(z + d, groups)}, device_id_type=MESH
        )
    for d in range(1, peers):
        pl.semaphore_signal(
            barrier, inc=1, device_id={"tensor": lax.rem(t + d, peers)}, device_id_type=MESH
        )

    loads = [pltpu.make_async_copy(up_hbm, up, load_sem.at[0])]
    loads.append(pltpu.make_async_copy(down_hbm, down, load_sem.at[1]))
    loads.append(pltpu.make_async_copy(x_hbm, x_all.at[z], load_sem.at[2]))
    for i in range(tiles):
        loads.append(
            pltpu.make_async_copy(
                w_hbm.at[:, pl.ds(i * w_all.shape[2], w_all.shape[2])],
                w_all.at[i],
                load_sem.at[3 + i],
            )
        )
    for copy in loads:
        copy.start()
    pl.semaphore_wait(barrier, groups + peers - 2)

    def x_copy(src, g, c, step):
        sems = x_right_sem if step > 0 else x_left_sem
        return pltpu.make_async_remote_copy(
            src_ref=src,
            dst_ref=x_all.at[g, c],
            send_sem=sems.at[g, c],
            recv_sem=x_recv_sem.at[g, c],
            device_id={"replica": z + step},
            device_id_type=MESH,
        )

    for c in range(chunks):
        @pl.when(z < groups - 1)
        def _():
            x_copy(x_hbm.at[c], z, c, 1).start()

        @pl.when(z > 0)
        def _():
            x_copy(x_hbm.at[c], z, c, -1).start()

    def up_copy(g):
        return pltpu.make_async_remote_copy(
            src_ref=up_send.at[g],
            dst_ref=up_got.at[t],
            send_sem=up_send_sem.at[g],
            recv_sem=up_recv_sem.at[t],
            device_id={"tensor": g},
            device_id_type=MESH,
        )

    loads[0].wait()

    @pl.loop(0, peers)
    def _(g):
        for j in range(cap):
            index = jnp.clip(table[g, t * cap + j] - t * owned, 0, owned - 1)
            up_send[g, j * rank : (j + 1) * rank, :] = up[index]

        @pl.when(g != t)
        def _():
            up_copy(g).start()

        @pl.when(g == t)
        def _():
            up_got[t] = up_send[g]

    loads[1].wait()

    @pl.loop(0, groups)
    def _(g):
        for j in range(cap):
            index = jnp.clip(table[g, z * cap + j] - z * owned, 0, owned - 1)
            down_sel[g, j * rank : (j + 1) * rank, :] = down[index]

    for copy in loads[2:]:
        copy.wait()

    def share_copy(g, c, i):
        return pltpu.make_async_remote_copy(
            src_ref=share_out.at[g, c, i],
            dst_ref=share_got.at[t, c, i],
            send_sem=share_send_sem.at[g, c, i],
            recv_sem=share_recv_sem.at[t, c, i],
            device_id={"tensor": g},
            device_id_type=MESH,
        )

    def rank_copy(g):
        return pltpu.make_async_remote_copy(
            src_ref=rank_out.at[g],
            dst_ref=rank_got.at[t],
            send_sem=rank_send_sem.at[g],
            recv_sem=rank_recv_sem.at[t],
            device_id={"tensor": g},
            device_id_type=MESH,
        )

    def work(g, c):
        @pl.when(c == chunks - 1)
        def _():
            block = x_all[g].reshape(chunks * rows, width)
            terms = lax.dot_general(
                down_sel[g], block, (((1,), (1,)), ((), ())), preferred_element_type=jnp.float32
            )
            slot = slots[g]
            total = jnp.zeros((rank, chunks * rows), jnp.float32)
            for j in range(cap):
                total += jnp.where(slot == z * cap + j, terms[j * rank : (j + 1) * rank, :], 0.0)

            @pl.when(g == t)
            def _():
                rank_got[t] = total

            @pl.when(g != t)
            def _():
                rank_out[g] = total
                rank_copy(g).start()

        @pl.loop(0, tiles)
        def _(i):
            share = jnp.dot(
                x_all[g, c], w_all[i], preferred_element_type=jnp.float32
            ).astype(jnp.bfloat16)

            @pl.when(g == t)
            def _():
                share_got[t, c, i] = share

            @pl.when(g != t)
            def _():
                share_out[g, c, i] = share
                share_copy(g, c, i).start()

    @pl.loop(0, chunks)
    def _(c):
        work(z, c)

    @pl.loop(0, (groups - 1) * chunks)
    def _(e):
        s = e // chunks + 1
        c = lax.rem(e, chunks)
        low, high = z - s, z + s

        @pl.when(low >= 0)
        def _():
            x_copy(x_hbm.at[0], low, c, 1).wait_recv()

            @pl.when(z < groups - 1)
            def _():
                x_copy(x_all.at[low, c], low, c, 1).start()

        @pl.when(high < groups)
        def _():
            x_copy(x_hbm.at[0], high, c, -1).wait_recv()

            @pl.when(z > 0)
            def _():
                x_copy(x_all.at[high, c], high, c, -1).start()

        @pl.loop(0, 2)
        def _(side):
            g = z - s + side * 2 * s

            @pl.when((g >= 0) & (g < groups))
            def _():
                work(g, c)

    for d in range(1, peers):
        src = lax.rem(t + d, peers)
        pltpu.make_async_copy(rank_got.at[src], rank_got.at[src], rank_recv_sem.at[src]).wait()
    total = rank_got[0]
    for i in range(1, peers):
        total += rank_got[i]
    fin_out[...] = total.astype(jnp.bfloat16)
    fin_got[z] = total.astype(jnp.bfloat16)

    def fin_copy(d):
        return pltpu.make_async_remote_copy(
            src_ref=fin_out,
            dst_ref=fin_got.at[z],
            send_sem=fin_send_sem.at[d],
            recv_sem=fin_recv_sem.at[z],
            device_id={"replica": lax.rem(z + d, groups)},
            device_id_type=MESH,
        )

    for d in range(1, groups):
        fin_copy(d).start()
    for d in range(1, peers):
        src = lax.rem(t + d, peers)
        pltpu.make_async_copy(up_got.at[src], up_got.at[src], up_recv_sem.at[src]).wait()
    for d in range(1, groups):
        src = lax.rem(z + d, groups)
        pltpu.make_async_copy(fin_got.at[src], fin_got.at[src], fin_recv_sem.at[src]).wait()
    shrink = fin_got[0].astype(jnp.float32)
    for i in range(1, groups):
        shrink += fin_got[i].astype(jnp.float32)
    slot = slots[t]
    spread = jnp.concatenate(
        [jnp.where(slot == s, shrink, 0.0) for s in range(groups * cap)], axis=0
    ).astype(jnp.bfloat16)
    span = w_all.shape[2]
    for i in range(tiles):
        factors = up_got[:, :, i * span : (i + 1) * span].reshape(peers * cap * rank, span)
        delta[i] = adapter_scale * lax.dot_general(
            spread, factors, (((0,), (0,)), ((), ())), preferred_element_type=jnp.float32
        )

    for c in range(chunks):
        for i in range(tiles):
            for d in range(1, peers):
                src = lax.rem(t + d, peers)
                pltpu.make_async_copy(
                    share_got.at[src, c, i], share_got.at[src, c, i], share_recv_sem.at[src, c, i]
                ).wait()
            base = share_got[0, c, i].astype(jnp.float32)
            for p in range(1, peers):
                base += share_got[p, c, i].astype(jnp.float32)
            out[c * rows : (c + 1) * rows, i * span : (i + 1) * span] = (
                base + delta[i, c * rows : (c + 1) * rows, :]
            ).astype(jnp.bfloat16)

    @pl.loop(0, groups)
    def _(g):
        @pl.loop(0, chunks)
        def _(c):
            @pl.when((g <= z) & (z < groups - 1))
            def _():
                x_copy(x_all.at[g, c], g, c, 1).wait_send()

            @pl.when((g >= z) & (z > 0))
            def _():
                x_copy(x_all.at[g, c], g, c, -1).wait_send()

            @pl.when(g != t)
            def _():
                for i in range(tiles):
                    share_copy(g, c, i).wait_send()

        @pl.when(g != t)
        def _():
            rank_copy(g).wait_send()
            up_copy(g).wait_send()

    for d in range(1, groups):
        fin_copy(d).wait_send()


def per_device(
    attention_rows,
    output_projection_weight,
    adapter_down_factors,
    adapter_up_factors,
    row_segment_slot,
    segment_slot_adapter,
):
    groups = lax.axis_size("replica")
    peers = lax.axis_size("tensor")
    row_count, width = attention_rows.shape
    columns = output_projection_weight.shape[1]
    rank = adapter_down_factors.shape[1]
    slot_rows = (segment_slot_adapter.shape[1] // groups) * rank
    chunks = row_count // row_chunk
    span = min(tile_width, columns)
    tiles = columns // span
    rows = attention_rows.reshape(chunks, row_chunk, width)
    slots = row_segment_slot.reshape(groups, 1, row_count)
    dma = pltpu.SemaphoreType.DMA
    bf16 = jnp.bfloat16
    hbm = pl.BlockSpec(memory_space=pl.ANY)
    vmem = pl.BlockSpec(memory_space=pltpu.VMEM)
    return pl.pallas_call(
        functools.partial(kernel, groups, peers, chunks, tiles),
        out_shape=jax.ShapeDtypeStruct((row_count, columns), bf16),
        in_specs=[pl.BlockSpec(memory_space=pltpu.SMEM), vmem, hbm, hbm, hbm, hbm],
        out_specs=vmem,
        scratch_shapes=[
            pltpu.VMEM((groups, chunks, row_chunk, width), bf16),
            pltpu.VMEM((tiles, width, span), bf16),
            pltpu.VMEM(adapter_down_factors.shape, bf16),
            pltpu.VMEM(adapter_up_factors.shape, bf16),
            pltpu.VMEM((groups, slot_rows, width), bf16),
            pltpu.VMEM((peers, slot_rows, columns), bf16),
            pltpu.VMEM((peers, slot_rows, columns), bf16),
            pltpu.VMEM((peers, chunks, tiles, row_chunk, span), bf16),
            pltpu.VMEM((peers, chunks, tiles, row_chunk, span), bf16),
            pltpu.VMEM((peers, rank, row_count), jnp.float32),
            pltpu.VMEM((peers, rank, row_count), jnp.float32),
            pltpu.VMEM((rank, row_count), bf16),
            pltpu.VMEM((groups, rank, row_count), bf16),
            pltpu.VMEM((tiles, row_count, span), jnp.float32),
            dma((3 + tiles,)),
            dma((groups, chunks)),
            dma((groups, chunks)),
            dma((groups, chunks)),
            dma((peers,)),
            dma((peers,)),
            dma((peers, chunks, tiles)),
            dma((peers, chunks, tiles)),
            dma((peers,)),
            dma((peers,)),
            dma((groups,)),
            dma((groups,)),
        ],
        compiler_params=pltpu.CompilerParams(
            collective_id=0, has_side_effects=True, vmem_limit_bytes=56 * 1024 * 1024
        ),
    )(
        segment_slot_adapter,
        slots,
        rows,
        output_projection_weight,
        adapter_down_factors,
        adapter_up_factors,
    )


def solution(mesh):
    return jax.shard_map(
        per_device,
        mesh=mesh,
        in_specs=(
            P(("parts", "replica"), "tensor"),
            P("tensor", "replica"),
            P("replica", None, "tensor"),
            P("tensor", None, "replica"),
            P("parts"),
            P("parts", None),
        ),
        out_specs=P(("parts", "tensor"), "replica"),
        check_vma=False,
    )
```

```python
import functools

import jax
import jax.numpy as jnp
from jax import lax
from jax.experimental import pallas as pl
from jax.experimental.pallas import tpu as pltpu
from jax.sharding import PartitionSpec as P

MESH = pl.DeviceIdType.MESH
adapter_scale = 2.0
row_chunk = 64
tile_width = 1024


def kernel(
    groups, peers, chunks, tiles,
    table, slots, x_hbm, w_hbm, down_hbm, up_hbm,
    out,
    x_all, w_all, down, up, down_sel, up_send, up_got,
    share_out, share_got, rank_out, rank_got, fin_out, fin_got, delta, far_sel,
    load_sem, x_right_sem, x_left_sem, x_recv_sem,
    up_send_sem, up_recv_sem, share_send_sem, share_recv_sem,
    rank_send_sem, rank_recv_sem, fin_send_sem, fin_recv_sem, far_sem,
):
    z = lax.axis_index("replica")
    t = lax.axis_index("tensor")
    owned, rank, width = down.shape
    cap = table.shape[1] // groups
    rows = x_all.shape[2]

    barrier = pltpu.get_barrier_semaphore()
    for d in range(1, groups):
        pl.semaphore_signal(
            barrier, inc=1, device_id={"replica": lax.rem(z + d, groups)}, device_id_type=MESH
        )
    for d in range(1, peers):
        pl.semaphore_signal(
            barrier, inc=1, device_id={"tensor": lax.rem(t + d, peers)}, device_id_type=MESH
        )

    loads = [pltpu.make_async_copy(up_hbm, up, load_sem.at[0])]
    loads.append(pltpu.make_async_copy(down_hbm, down, load_sem.at[1]))
    loads.append(pltpu.make_async_copy(x_hbm, x_all.at[z], load_sem.at[2]))
    for i in range(tiles):
        loads.append(
            pltpu.make_async_copy(
                w_hbm.at[:, pl.ds(i * w_all.shape[2], w_all.shape[2])],
                w_all.at[i],
                load_sem.at[3 + i],
            )
        )
    for copy in loads:
        copy.start()
    pl.semaphore_wait(barrier, groups + peers - 2)

    def x_copy(src, g, c, step):
        sems = x_right_sem if step > 0 else x_left_sem
        return pltpu.make_async_remote_copy(
            src_ref=src,
            dst_ref=x_all.at[g, c],
            send_sem=sems.at[g, c],
            recv_sem=x_recv_sem.at[g, c],
            device_id={"replica": z + step},
            device_id_type=MESH,
        )

    for c in range(chunks):
        @pl.when(z < groups - 1)
        def _():
            x_copy(x_hbm.at[c], z, c, 1).start()

        @pl.when(z > 0)
        def _():
            x_copy(x_hbm.at[c], z, c, -1).start()

    def up_copy(g):
        return pltpu.make_async_remote_copy(
            src_ref=up_send.at[g],
            dst_ref=up_got.at[t],
            send_sem=up_send_sem.at[g],
            recv_sem=up_recv_sem.at[t],
            device_id={"tensor": g},
            device_id_type=MESH,
        )

    loads[0].wait()

    @pl.loop(0, peers)
    def _(g):
        for j in range(cap):
            index = jnp.clip(table[g, t * cap + j] - t * owned, 0, owned - 1)
            up_send[g, j * rank : (j + 1) * rank, :] = up[index]

        @pl.when(g != t)
        def _():
            up_copy(g).start()

        @pl.when(g == t)
        def _():
            up_got[t] = up_send[g]

    loads[1].wait()

    @pl.loop(0, groups)
    def _(g):
        for j in range(cap):
            index = jnp.clip(table[g, z * cap + j] - z * owned, 0, owned - 1)
            down_sel[g, j * rank : (j + 1) * rank, :] = down[index]

    last = groups - 1
    at_end = (z == 0) | (z == last)

    def far_copy(g, target):
        return pltpu.make_async_remote_copy(
            src_ref=down_sel.at[g],
            dst_ref=far_sel,
            send_sem=far_sem.at[0],
            recv_sem=far_sem.at[1],
            device_id={"replica": target},
            device_id_type=MESH,
        )

    @pl.when(z == 0)
    def _():
        far_copy(last, 1).start()

    @pl.when(z == last)
    def _():
        far_copy(0, last - 1).start()

    for copy in loads[2:]:
        copy.wait()

    def share_copy(g, c, i):
        return pltpu.make_async_remote_copy(
            src_ref=share_out.at[g, c, i],
            dst_ref=share_got.at[t, c, i],
            send_sem=share_send_sem.at[g, c, i],
            recv_sem=share_recv_sem.at[t, c, i],
            device_id={"tensor": g},
            device_id_type=MESH,
        )

    def rank_copy(g):
        return pltpu.make_async_remote_copy(
            src_ref=rank_out.at[g],
            dst_ref=rank_got.at[t],
            send_sem=rank_send_sem.at[g],
            recv_sem=rank_recv_sem.at[t],
            device_id={"tensor": g},
            device_id_type=MESH,
        )

    def put_rank(g, total):
        @pl.when(g == t)
        def _():
            rank_got[t] = total

        @pl.when(g != t)
        def _():
            rank_out[g] = total
            rank_copy(g).start()

    def rank_terms(factors, g, owner):
        block = x_all[g].reshape(chunks * rows, width)
        terms = lax.dot_general(
            factors, block, (((1,), (1,)), ((), ())), preferred_element_type=jnp.float32
        )
        slot = slots[g]
        total = jnp.zeros((rank, chunks * rows), jnp.float32)
        for j in range(cap):
            total += jnp.where(slot == owner * cap + j, terms[j * rank : (j + 1) * rank, :], 0.0)
        return total

    @pl.when(at_end)
    def _():
        put_rank(last - z, jnp.zeros((rank, chunks * rows), jnp.float32))

    def work(g, c):
        beside = ((z == 1) & (g == last)) | ((z == last - 1) & (g == 0))
        done = (c == chunks - 1) & ~(at_end & (g == last - z))

        @pl.when(done & ~beside)
        def _():
            put_rank(g, rank_terms(down_sel[g], g, z))

        @pl.when(done & beside)
        def _():
            far_copy(0, z).wait_recv()
            put_rank(
                g,
                rank_terms(down_sel[g], g, z) + rank_terms(far_sel[...], g, last - g),
            )

        @pl.loop(0, tiles)
        def _(i):
            share = jnp.dot(
                x_all[g, c], w_all[i], preferred_element_type=jnp.float32
            ).astype(jnp.bfloat16)

            @pl.when(g == t)
            def _():
                share_got[t, c, i] = share

            @pl.when(g != t)
            def _():
                share_out[g, c, i] = share
                share_copy(g, c, i).start()

    @pl.loop(0, chunks)
    def _(c):
        work(z, c)

    def event(e):
        s = e // chunks + 1
        c = lax.rem(e, chunks)
        low, high = z - s, z + s

        @pl.when(low >= 0)
        def _():
            x_copy(x_hbm.at[0], low, c, 1).wait_recv()

            @pl.when(z < groups - 1)
            def _():
                x_copy(x_all.at[low, c], low, c, 1).start()

        @pl.when(high < groups)
        def _():
            x_copy(x_hbm.at[0], high, c, -1).wait_recv()

            @pl.when(z > 0)
            def _():
                x_copy(x_all.at[high, c], high, c, -1).start()

        @pl.loop(0, 2)
        def _(side):
            g = z - s + side * 2 * s

            @pl.when((g >= 0) & (g < groups))
            def _():
                work(g, c)

    @pl.loop(0, (groups - 2) * chunks)
    def _(e):
        event(e)

    for d in range(1, peers):
        src = lax.rem(t + d, peers)
        pltpu.make_async_copy(rank_got.at[src], rank_got.at[src], rank_recv_sem.at[src]).wait()
    total = rank_got[0]
    for i in range(1, peers):
        total += rank_got[i]
    fin_out[...] = total.astype(jnp.bfloat16)
    fin_got[z] = total.astype(jnp.bfloat16)

    def fin_copy(d):
        return pltpu.make_async_remote_copy(
            src_ref=fin_out,
            dst_ref=fin_got.at[z],
            send_sem=fin_send_sem.at[d],
            recv_sem=fin_recv_sem.at[z],
            device_id={"replica": lax.rem(z + d, groups)},
            device_id_type=MESH,
        )

    for d in range(1, groups):
        fin_copy(d).start()

    @pl.loop((groups - 2) * chunks, (groups - 1) * chunks - 1)
    def _(e):
        event(e)

    for d in range(1, peers):
        src = lax.rem(t + d, peers)
        pltpu.make_async_copy(up_got.at[src], up_got.at[src], up_recv_sem.at[src]).wait()
    for d in range(1, groups):
        src = lax.rem(z + d, groups)
        pltpu.make_async_copy(fin_got.at[src], fin_got.at[src], fin_recv_sem.at[src]).wait()
    shrink = fin_got[0].astype(jnp.float32)
    for i in range(1, groups):
        shrink += fin_got[i].astype(jnp.float32)
    slot = slots[t]
    spread = jnp.concatenate(
        [jnp.where(slot == s, shrink, 0.0) for s in range(groups * cap)], axis=0
    ).astype(jnp.bfloat16)
    span = w_all.shape[2]
    for i in range(tiles):
        factors = up_got[:, :, i * span : (i + 1) * span].reshape(peers * cap * rank, span)
        delta[i] = adapter_scale * lax.dot_general(
            spread, factors, (((0,), (0,)), ((), ())), preferred_element_type=jnp.float32
        )

    def combine(c):
        for i in range(tiles):
            for d in range(1, peers):
                src = lax.rem(t + d, peers)
                pltpu.make_async_copy(
                    share_got.at[src, c, i], share_got.at[src, c, i], share_recv_sem.at[src, c, i]
                ).wait()
            base = share_got[0, c, i].astype(jnp.float32)
            for p in range(1, peers):
                base += share_got[p, c, i].astype(jnp.float32)
            out[c * rows : (c + 1) * rows, i * span : (i + 1) * span] = (
                base + delta[i, c * rows : (c + 1) * rows, :]
            ).astype(jnp.bfloat16)

    for c in range(chunks - 2):
        combine(c)

    @pl.loop((groups - 1) * chunks - 1, (groups - 1) * chunks)
    def _(e):
        event(e)

    for c in range(chunks - 2, chunks):
        combine(c)

    @pl.loop(0, groups)
    def _(g):
        @pl.loop(0, chunks)
        def _(c):
            @pl.when((g <= z) & (z < groups - 1))
            def _():
                x_copy(x_all.at[g, c], g, c, 1).wait_send()

            @pl.when((g >= z) & (z > 0))
            def _():
                x_copy(x_all.at[g, c], g, c, -1).wait_send()

            @pl.when(g != t)
            def _():
                for i in range(tiles):
                    share_copy(g, c, i).wait_send()

        @pl.when(g != t)
        def _():
            rank_copy(g).wait_send()
            up_copy(g).wait_send()

    @pl.when(at_end)
    def _():
        far_copy(0, z).wait_send()

    for d in range(1, groups):
        fin_copy(d).wait_send()


def per_device(
    attention_rows,
    output_projection_weight,
    adapter_down_factors,
    adapter_up_factors,
    row_segment_slot,
    segment_slot_adapter,
):
    groups = lax.axis_size("replica")
    peers = lax.axis_size("tensor")
    row_count, width = attention_rows.shape
    columns = output_projection_weight.shape[1]
    rank = adapter_down_factors.shape[1]
    slot_rows = (segment_slot_adapter.shape[1] // groups) * rank
    chunks = row_count // row_chunk
    span = min(tile_width, columns)
    tiles = columns // span
    rows = attention_rows.reshape(chunks, row_chunk, width)
    slots = row_segment_slot.reshape(groups, 1, row_count)
    dma = pltpu.SemaphoreType.DMA
    bf16 = jnp.bfloat16
    hbm = pl.BlockSpec(memory_space=pl.ANY)
    vmem = pl.BlockSpec(memory_space=pltpu.VMEM)
    return pl.pallas_call(
        functools.partial(kernel, groups, peers, chunks, tiles),
        out_shape=pltpu.VMEM((row_count, columns), bf16),
        in_specs=[pl.BlockSpec(memory_space=pltpu.SMEM), vmem, hbm, hbm, hbm, hbm],
        out_specs=vmem,
        scratch_shapes=[
            pltpu.VMEM((groups, chunks, row_chunk, width), bf16),
            pltpu.VMEM((tiles, width, span), bf16),
            pltpu.VMEM(adapter_down_factors.shape, bf16),
            pltpu.VMEM(adapter_up_factors.shape, bf16),
            pltpu.VMEM((groups, slot_rows, width), bf16),
            pltpu.VMEM((peers, slot_rows, columns), bf16),
            pltpu.VMEM((peers, slot_rows, columns), bf16),
            pltpu.VMEM((peers, chunks, tiles, row_chunk, span), bf16),
            pltpu.VMEM((peers, chunks, tiles, row_chunk, span), bf16),
            pltpu.VMEM((peers, rank, row_count), jnp.float32),
            pltpu.VMEM((peers, rank, row_count), jnp.float32),
            pltpu.VMEM((rank, row_count), bf16),
            pltpu.VMEM((groups, rank, row_count), bf16),
            pltpu.VMEM((tiles, row_count, span), jnp.float32),
            pltpu.VMEM((slot_rows, width), bf16),
            dma((3 + tiles,)),
            dma((groups, chunks)),
            dma((groups, chunks)),
            dma((groups, chunks)),
            dma((peers,)),
            dma((peers,)),
            dma((peers, chunks, tiles)),
            dma((peers, chunks, tiles)),
            dma((peers,)),
            dma((peers,)),
            dma((groups,)),
            dma((groups,)),
            dma((2,)),
        ],
        compiler_params=pltpu.CompilerParams(
            collective_id=0, has_side_effects=True, vmem_limit_bytes=56 * 1024 * 1024
        ),
    )(
        segment_slot_adapter,
        slots,
        rows,
        output_projection_weight,
        adapter_down_factors,
        adapter_up_factors,
    )


def solution(mesh):
    return jax.shard_map(
        per_device,
        mesh=mesh,
        in_specs=(
            P(("parts", "replica"), "tensor"),
            P("tensor", "replica"),
            P("replica", None, "tensor"),
            P("tensor", None, "replica"),
            P("parts"),
            P("parts", None),
        ),
        out_specs=P(("parts", "tensor"), "replica"),
        check_vma=False,
    )
```

```python
import functools

import jax
import jax.numpy as jnp
from jax import lax
from jax.experimental import pallas as pl
from jax.experimental.pallas import tpu as pltpu
from jax.sharding import PartitionSpec as P

MESH = pl.DeviceIdType.MESH
adapter_scale = 2.0
row_chunk = 64
tile_width = 2048


def kernel(
    groups, peers, chunks, tiles,
    table, slots, x_hbm, w_hbm, down_hbm, up_hbm,
    out,
    x_all, w_all, down, up, down_sel, up_send, up_got,
    share_out, share_got, rank_out, rank_got, fin_out, fin_got, delta, far_sel,
    load_sem, x_right_sem, x_left_sem, x_recv_sem,
    up_send_sem, up_recv_sem, share_send_sem, share_recv_sem,
    rank_send_sem, rank_recv_sem, fin_send_sem, fin_recv_sem, far_sem, half_sem,
):
    z = lax.axis_index("replica")
    t = lax.axis_index("tensor")
    owned, rank, width = down.shape
    cap = table.shape[1] // groups
    rows = x_all.shape[2]

    barrier = pltpu.get_barrier_semaphore()
    for d in range(1, groups):
        pl.semaphore_signal(
            barrier, inc=1, device_id={"replica": lax.rem(z + d, groups)}, device_id_type=MESH
        )
    for d in range(1, peers):
        pl.semaphore_signal(
            barrier, inc=1, device_id={"tensor": lax.rem(t + d, peers)}, device_id_type=MESH
        )

    loads = [pltpu.make_async_copy(up_hbm, up, load_sem.at[0])]
    loads.append(pltpu.make_async_copy(down_hbm, down, load_sem.at[1]))
    loads.append(pltpu.make_async_copy(x_hbm, x_all.at[z], load_sem.at[2]))
    for i in range(tiles):
        loads.append(
            pltpu.make_async_copy(
                w_hbm.at[:, pl.ds(i * w_all.shape[2], w_all.shape[2])],
                w_all.at[i],
                load_sem.at[3 + i],
            )
        )
    for copy in loads:
        copy.start()
    pl.semaphore_wait(barrier, groups + peers - 2)

    def x_copy(src, g, c, step):
        sems = x_right_sem if step > 0 else x_left_sem
        return pltpu.make_async_remote_copy(
            src_ref=src,
            dst_ref=x_all.at[g, c],
            send_sem=sems.at[g, c],
            recv_sem=x_recv_sem.at[g, c],
            device_id={"replica": z + step},
            device_id_type=MESH,
        )

    half = rows // 2
    tail = chunks - 1

    def x_half(g, step, h):
        sems = x_right_sem if step > 0 else x_left_sem
        return pltpu.make_async_remote_copy(
            src_ref=x_all.at[g, tail, pl.ds(h * half, half)],
            dst_ref=x_all.at[g, tail, pl.ds(h * half, half)],
            send_sem=sems.at[g, tail],
            recv_sem=half_sem.at[h],
            device_id={"replica": z + step},
            device_id_type=MESH,
        )

    for c in range(chunks):
        @pl.when(z < groups - 1)
        def _():
            x_copy(x_hbm.at[c], z, c, 1).start()

        @pl.when(z > 0)
        def _():
            x_copy(x_hbm.at[c], z, c, -1).start()

    def up_copy(g):
        return pltpu.make_async_remote_copy(
            src_ref=up_send.at[g],
            dst_ref=up_got.at[t],
            send_sem=up_send_sem.at[g],
            recv_sem=up_recv_sem.at[t],
            device_id={"tensor": g},
            device_id_type=MESH,
        )

    loads[0].wait()

    @pl.loop(0, peers)
    def _(g):
        for j in range(cap):
            index = jnp.clip(table[g, t * cap + j] - t * owned, 0, owned - 1)
            up_send[g, j * rank : (j + 1) * rank, :] = up[index]

        @pl.when(g != t)
        def _():
            up_copy(g).start()

        @pl.when(g == t)
        def _():
            up_got[t] = up_send[g]

    loads[1].wait()

    @pl.loop(0, groups)
    def _(g):
        for j in range(cap):
            index = jnp.clip(table[g, z * cap + j] - z * owned, 0, owned - 1)
            down_sel[g, j * rank : (j + 1) * rank, :] = down[index]

    last = groups - 1
    at_end = (z == 0) | (z == last)

    def far_copy(g, target):
        return pltpu.make_async_remote_copy(
            src_ref=down_sel.at[g],
            dst_ref=far_sel,
            send_sem=far_sem.at[0],
            recv_sem=far_sem.at[1],
            device_id={"replica": target},
            device_id_type=MESH,
        )

    @pl.when(z == 0)
    def _():
        far_copy(last, 1).start()

    @pl.when(z == last)
    def _():
        far_copy(0, last - 1).start()

    for copy in loads[2:]:
        copy.wait()

    def share_copy(g, c, i):
        return pltpu.make_async_remote_copy(
            src_ref=share_out.at[g, c, i],
            dst_ref=share_got.at[t, c, i],
            send_sem=share_send_sem.at[g, c, i],
            recv_sem=share_recv_sem.at[t, c, i],
            device_id={"tensor": g},
            device_id_type=MESH,
        )

    def rank_copy(g):
        return pltpu.make_async_remote_copy(
            src_ref=rank_out.at[g],
            dst_ref=rank_got.at[t],
            send_sem=rank_send_sem.at[g],
            recv_sem=rank_recv_sem.at[t],
            device_id={"tensor": g},
            device_id_type=MESH,
        )

    def put_rank(g, total):
        @pl.when(g == t)
        def _():
            rank_got[t] = total

        @pl.when(g != t)
        def _():
            rank_out[g] = total
            rank_copy(g).start()

    def rank_terms(factors, g, owner):
        block = x_all[g].reshape(chunks * rows, width)
        terms = lax.dot_general(
            factors, block, (((1,), (1,)), ((), ())), preferred_element_type=jnp.float32
        )
        slot = slots[g]
        total = jnp.zeros((rank, chunks * rows), jnp.float32)
        for j in range(cap):
            total += jnp.where(slot == owner * cap + j, terms[j * rank : (j + 1) * rank, :], 0.0)
        return total

    @pl.when(at_end)
    def _():
        put_rank(last - z, jnp.zeros((rank, chunks * rows), jnp.float32))

    def work(g, c):
        beside = ((z == 1) & (g == last)) | ((z == last - 1) & (g == 0))
        done = (c == chunks - 1) & ~(at_end & (g == last - z))

        @pl.when(done & ~beside)
        def _():
            put_rank(g, rank_terms(down_sel[g], g, z))

        @pl.when(done & beside)
        def _():
            far_copy(0, z).wait_recv()
            put_rank(
                g,
                rank_terms(down_sel[g], g, z) + rank_terms(far_sel[...], g, last - g),
            )

        @pl.loop(0, tiles)
        def _(i):
            share = jnp.dot(
                x_all[g, c], w_all[i], preferred_element_type=jnp.float32
            ).astype(jnp.bfloat16)

            @pl.when(g == t)
            def _():
                share_got[t, c, i] = share

            @pl.when(g != t)
            def _():
                share_out[g, c, i] = share
                share_copy(g, c, i).start()

    @pl.loop(0, chunks)
    def _(c):
        work(z, c)

    def event(e):
        s = e // chunks + 1
        c = lax.rem(e, chunks)
        low, high = z - s, z + s

        @pl.when(low >= 0)
        def _():
            x_copy(x_hbm.at[0], low, c, 1).wait_recv()

            split = (c == tail) & (z == last - 1) & (low == 0)

            @pl.when((z < last) & ~split)
            def _():
                x_copy(x_all.at[low, c], low, c, 1).start()

            @pl.when(split)
            def _():
                for h in range(2):
                    x_half(low, 1, h).start()

        @pl.when(high < groups)
        def _():
            x_copy(x_hbm.at[0], high, c, -1).wait_recv()

            split = (c == tail) & (z == 1) & (high == last)

            @pl.when((z > 0) & ~split)
            def _():
                x_copy(x_all.at[high, c], high, c, -1).start()

            @pl.when(split)
            def _():
                for h in range(2):
                    x_half(high, -1, h).start()

        @pl.loop(0, 2)
        def _(side):
            g = z - s + side * 2 * s

            @pl.when((g >= 0) & (g < groups))
            def _():
                work(g, c)

    @pl.loop(0, (groups - 2) * chunks)
    def _(e):
        event(e)

    for d in range(1, peers):
        src = lax.rem(t + d, peers)
        pltpu.make_async_copy(rank_got.at[src], rank_got.at[src], rank_recv_sem.at[src]).wait()
    total = rank_got[0]
    for i in range(1, peers):
        total += rank_got[i]
    fin_out[...] = total.astype(jnp.bfloat16)
    fin_got[z] = total.astype(jnp.bfloat16)

    def fin_copy(d):
        return pltpu.make_async_remote_copy(
            src_ref=fin_out,
            dst_ref=fin_got.at[z],
            send_sem=fin_send_sem.at[d],
            recv_sem=fin_recv_sem.at[z],
            device_id={"replica": lax.rem(z + d, groups)},
            device_id_type=MESH,
        )

    for d in range(1, groups):
        fin_copy(d).start()

    @pl.loop((groups - 2) * chunks, (groups - 1) * chunks - 1)
    def _(e):
        event(e)

    for d in range(1, peers):
        src = lax.rem(t + d, peers)
        pltpu.make_async_copy(up_got.at[src], up_got.at[src], up_recv_sem.at[src]).wait()
    for d in range(1, groups):
        src = lax.rem(z + d, groups)
        pltpu.make_async_copy(fin_got.at[src], fin_got.at[src], fin_recv_sem.at[src]).wait()
    shrink = fin_got[0].astype(jnp.float32)
    for i in range(1, groups):
        shrink += fin_got[i].astype(jnp.float32)
    slot = slots[t]
    spread = jnp.concatenate(
        [jnp.where(slot == s, shrink, 0.0) for s in range(groups * cap)], axis=0
    ).astype(jnp.bfloat16)
    span = w_all.shape[2]
    for i in range(tiles):
        factors = up_got[:, :, i * span : (i + 1) * span].reshape(peers * cap * rank, span)
        delta[i] = adapter_scale * lax.dot_general(
            spread, factors, (((0,), (0,)), ((), ())), preferred_element_type=jnp.float32
        )

    def combine(c):
        for i in range(tiles):
            for d in range(1, peers):
                src = lax.rem(t + d, peers)
                pltpu.make_async_copy(
                    share_got.at[src, c, i], share_got.at[src, c, i], share_recv_sem.at[src, c, i]
                ).wait()
            base = share_got[0, c, i].astype(jnp.float32)
            for p in range(1, peers):
                base += share_got[p, c, i].astype(jnp.float32)
            out[c * rows : (c + 1) * rows, i * span : (i + 1) * span] = (
                base + delta[i, c * rows : (c + 1) * rows, :]
            ).astype(jnp.bfloat16)

    for c in range(chunks - 2):
        combine(c)

    def half_share(g, i, h):
        return pltpu.make_async_remote_copy(
            src_ref=share_out.at[g, tail, i, pl.ds(h * half, half)],
            dst_ref=share_got.at[t, tail, i, pl.ds(h * half, half)],
            send_sem=share_send_sem.at[g, tail, i],
            recv_sem=share_recv_sem.at[t, tail, i],
            device_id={"tensor": g},
            device_id_type=MESH,
        )

    @pl.when(at_end)
    def _():
        g = last - z
        for h in range(2):
            x_half(g, 1, h).wait_recv()
            part = slice(h * half, (h + 1) * half)

            @pl.loop(0, tiles)
            def _(i):
                share = jnp.dot(
                    x_all[g, tail, part, :], w_all[i], preferred_element_type=jnp.float32
                ).astype(jnp.bfloat16)

                @pl.when(g == t)
                def _():
                    share_got[t, tail, i, part, :] = share

                @pl.when(g != t)
                def _():
                    share_out[g, tail, i, part, :] = share
                    half_share(g, i, h).start()

    for c in range(chunks - 2, chunks):
        combine(c)

    @pl.loop(0, groups)
    def _(g):
        @pl.loop(0, chunks)
        def _(c):
            @pl.when((g <= z) & (z < groups - 1))
            def _():
                x_copy(x_all.at[g, c], g, c, 1).wait_send()

            @pl.when((g >= z) & (z > 0))
            def _():
                x_copy(x_all.at[g, c], g, c, -1).wait_send()

            @pl.when(g != t)
            def _():
                for i in range(tiles):
                    share_copy(g, c, i).wait_send()

        @pl.when(g != t)
        def _():
            rank_copy(g).wait_send()
            up_copy(g).wait_send()

    @pl.when(at_end)
    def _():
        far_copy(0, z).wait_send()

    for d in range(1, groups):
        fin_copy(d).wait_send()


def per_device(
    attention_rows,
    output_projection_weight,
    adapter_down_factors,
    adapter_up_factors,
    row_segment_slot,
    segment_slot_adapter,
):
    groups = lax.axis_size("replica")
    peers = lax.axis_size("tensor")
    row_count, width = attention_rows.shape
    columns = output_projection_weight.shape[1]
    rank = adapter_down_factors.shape[1]
    slot_rows = (segment_slot_adapter.shape[1] // groups) * rank
    chunks = row_count // row_chunk
    span = min(tile_width, columns)
    tiles = columns // span
    rows = attention_rows.reshape(chunks, row_chunk, width)
    slots = row_segment_slot.reshape(groups, 1, row_count)
    dma = pltpu.SemaphoreType.DMA
    bf16 = jnp.bfloat16
    hbm = pl.BlockSpec(memory_space=pl.ANY)
    vmem = pl.BlockSpec(memory_space=pltpu.VMEM)
    return pl.pallas_call(
        functools.partial(kernel, groups, peers, chunks, tiles),
        out_shape=pltpu.VMEM((row_count, columns), bf16),
        in_specs=[pl.BlockSpec(memory_space=pltpu.SMEM), vmem, hbm, hbm, hbm, hbm],
        out_specs=vmem,
        scratch_shapes=[
            pltpu.VMEM((groups, chunks, row_chunk, width), bf16),
            pltpu.VMEM((tiles, width, span), bf16),
            pltpu.VMEM(adapter_down_factors.shape, bf16),
            pltpu.VMEM(adapter_up_factors.shape, bf16),
            pltpu.VMEM((groups, slot_rows, width), bf16),
            pltpu.VMEM((peers, slot_rows, columns), bf16),
            pltpu.VMEM((peers, slot_rows, columns), bf16),
            pltpu.VMEM((peers, chunks, tiles, row_chunk, span), bf16),
            pltpu.VMEM((peers, chunks, tiles, row_chunk, span), bf16),
            pltpu.VMEM((peers, rank, row_count), jnp.float32),
            pltpu.VMEM((peers, rank, row_count), jnp.float32),
            pltpu.VMEM((rank, row_count), bf16),
            pltpu.VMEM((groups, rank, row_count), bf16),
            pltpu.VMEM((tiles, row_count, span), jnp.float32),
            pltpu.VMEM((slot_rows, width), bf16),
            dma((3 + tiles,)),
            dma((groups, chunks)),
            dma((groups, chunks)),
            dma((groups, chunks)),
            dma((peers,)),
            dma((peers,)),
            dma((peers, chunks, tiles)),
            dma((peers, chunks, tiles)),
            dma((peers,)),
            dma((peers,)),
            dma((groups,)),
            dma((groups,)),
            dma((2,)),
            dma((2,)),
        ],
        compiler_params=pltpu.CompilerParams(
            collective_id=0, has_side_effects=True, vmem_limit_bytes=56 * 1024 * 1024
        ),
    )(
        segment_slot_adapter,
        slots,
        rows,
        output_projection_weight,
        adapter_down_factors,
        adapter_up_factors,
    )


def solution(mesh):
    return jax.shard_map(
        per_device,
        mesh=mesh,
        in_specs=(
            P(("parts", "replica"), "tensor"),
            P("tensor", "replica"),
            P("replica", None, "tensor"),
            P("tensor", None, "replica"),
            P("parts"),
            P("parts", None),
        ),
        out_specs=P(("parts", "tensor"), "replica"),
        check_vma=False,
    )
```
